32 devices in a mesh: facet: 8 (over y, x, core), col: 4 (over z).
Axes of the slice: x: 2, y: 2, z: 4, core: 2. Of those that a mesh axis runs over, the one named last changes fastest.
Arguments:
- strips: float32 [8, 2, 192, 2048], P('facet', None, 'col'), may hold values from -6 to 6
- sub_offset: int32 [4, 8], replicated, may hold values from 0 to 2047
- uv_cells: int32 [4, 8, 2, 128], P('col', 'facet'), may hold values from 0 to 255
- measured: float32 [4, 8, 2, 128], P('col', 'facet'), may hold values from -6 to 6
Outputs:
- dirty_image: float32 [8, 2, 192, 2048], P('facet', None, 'col')
- residual_vis: float32 [4, 8, 2, 128], P('col', 'facet')
The draws below stay inside these ranges and needn't reach their ends.
All inputs are finite; a program needn't handle non-finite values.
Results may differ from the reference program's by a relative error of at most 0.0003.
Values sent between devices are 32-bit elements; how exact they have to be, the bound alone decides.
A program may use at most 64 MiB of HBM per device.

```python
import math
import jax
import jax.numpy as jnp
from jax import lax

CONTRIB_WIDTH = 48
FACET_STRIP_LEN = 2048
SUBGRID_SIZE = 256
VIS_PER_SUBGRID = 128
FACETS = 8
COLS = 4
FR = 192
SG_COL = 8
SUBGRID_TOTAL = 32
N_FACET = 8


def with_ends(entries, stream_key, low, high):
    spot = [jax.random.randint(jax.random.fold_in(stream_key, axis), (), 0, length) for axis, length in enumerate(entries.shape)]
    longest = entries.shape.index(max(entries.shape))
    beside = spot[:longest] + [(spot[longest] + 1) % entries.shape[longest]] + spot[longest + 1:]
    return entries.at[tuple(spot)].set(low).at[tuple(beside)].set(high)


def level_of(own_key, dims, shards, low, largest):
    gain, own = 1.0, jax.random.fold_in(own_key, 6)
    for position, parts in shards:
        steps = jnp.exp(jax.random.uniform(jax.random.fold_in(own, position), (parts,), jnp.float32, low / len(shards), largest / len(shards)))
        gain = gain * jnp.repeat(steps, dims[position] // parts).reshape([-1 if axis == position else 1 for axis in range(len(dims))])
    return gain


def bell_draw(rng, dims, deviation, bound, shards=(), held_as=jnp.bfloat16):
    loudness = level_of(rng, dims, shards, -0.22, 0.18) if shards else 1.0
    entries = jax.random.normal(rng, dims, jnp.float32) * deviation * loudness
    return jnp.minimum(jnp.maximum(entries, -bound), bound).astype(held_as)


def setup_inputs(seed: int = 0) -> dict:
    splits = jax.random.split(jax.random.key(seed), 5)
    strips = bell_draw(splits[0], (FACETS, 2, FR, FACET_STRIP_LEN), 1.0, 6.0, ((0, 8), (2, 4)), jnp.float32)
    sub_offset = with_ends(jax.random.randint(splits[1], (COLS, SG_COL), 0, FACET_STRIP_LEN), jax.random.fold_in(splits[1], 1), 0, FACET_STRIP_LEN - 1).astype(jnp.int32)
    uv_cells = with_ends(jax.random.randint(splits[2], (COLS, SG_COL, 2, VIS_PER_SUBGRID), 0, SUBGRID_SIZE), jax.random.fold_in(splits[2], 1), 0, SUBGRID_SIZE - 1).astype(jnp.int32)
    measured = bell_draw(splits[3], (COLS, SG_COL, 2, VIS_PER_SUBGRID), 1.0, 6.0, ((0, 4), (1, 8)), jnp.float32)
    return dict(strips=strips, sub_offset=sub_offset, uv_cells=uv_cells, measured=measured)


def complex_product(ar, ai, br, bi):
    high_precision = lax.Precision.HIGHEST
    rr = jnp.dot(ar, br, precision=high_precision, preferred_element_type=jnp.float32) - jnp.dot(ai, bi, precision=high_precision, preferred_element_type=jnp.float32)
    ri = jnp.dot(ar, bi, precision=high_precision, preferred_element_type=jnp.float32) + jnp.dot(ai, br, precision=high_precision, preferred_element_type=jnp.float32)
    return (rr, ri)

def phase_terms(numer, denom):
    angle = (numer % denom).astype(jnp.float32) * (2.0 * math.pi / denom)
    return (jnp.cos(angle), jnp.sin(angle))

def facet_strip_kernel(grid_offset, strip_width, strip_length):
    rows = jnp.arange(strip_length, dtype=jnp.int32)[:, None]
    cols = jnp.arange(strip_width, dtype=jnp.int32)[None, :]
    cosine, sine = phase_terms(rows * (grid_offset + cols), strip_length)
    norm = 1.0 / math.sqrt(strip_length)
    return (cosine * norm, -sine * norm)

def einsum_hi(form, left, right):
    return jnp.einsum(form, left, right, precision=lax.Precision.HIGHEST)

def subgrid_update(kernel_real, kernel_imaginary, u_coordinates, v_coordinates, measured_real, measured_imaginary, facet_count):
    strip_width = kernel_real.shape[-1]
    total = strip_width * facet_count
    factor = (facet_count * strip_width * strip_width) ** (-0.25)
    grid_cells = jnp.arange(SUBGRID_SIZE, dtype=jnp.int32)
    cosine, sine = phase_terms(grid_cells[:, None] * jnp.arange(total, dtype=jnp.int32)[None, :], total)
    ere = factor * cosine
    eim = factor * sine
    ebre = ere.reshape(SUBGRID_SIZE, facet_count, strip_width)
    ebim = eim.reshape(SUBGRID_SIZE, facet_count, strip_width)
    are = einsum_hi('ufk,fkl->ufl', ebre, kernel_real) - einsum_hi('ufk,fkl->ufl', ebim, kernel_imaginary)
    aim = einsum_hi('ufk,fkl->ufl', ebre, kernel_imaginary) + einsum_hi('ufk,fkl->ufl', ebim, kernel_real)
    sre, sim = complex_product(are.reshape(SUBGRID_SIZE, total), aim.reshape(SUBGRID_SIZE, total), ere.T, eim.T)
    ucos, usin = phase_terms(u_coordinates[:, None] * grid_cells[None, :], SUBGRID_SIZE)
    v_cosine, v_sine = phase_terms(v_coordinates[:, None] * grid_cells[None, :], SUBGRID_SIZE)
    fure, fuim = (ucos, -usin)
    fvre, fvim = (v_cosine, -v_sine)
    tre, tim = complex_product(fure, fuim, sre, sim)
    pred_re = lax.optimization_barrier(jnp.sum(tre * fvre - tim * fvim, axis=1)) / SUBGRID_SIZE
    pred_im = lax.optimization_barrier(jnp.sum(tre * fvim + tim * fvre, axis=1)) / SUBGRID_SIZE
    residual_real = measured_real - pred_re
    residual_imaginary = measured_imaginary - pred_im
    gre = fvre * residual_real[:, None] + fvim * residual_imaginary[:, None]
    gim = fvre * residual_imaginary[:, None] - fvim * residual_real[:, None]
    spre, spim = complex_product(fure.T, -fuim.T, gre, gim)
    bre, bim = complex_product(ere.T, -eim.T, spre, spim)
    bre = bre.reshape(facet_count, strip_width, SUBGRID_SIZE)
    bim = bim.reshape(facet_count, strip_width, SUBGRID_SIZE)
    kernel_phase_real = einsum_hi('fka,afl->fkl', bre, ebre) + einsum_hi('fka,afl->fkl', bim, ebim)
    kernel_phase_imaginary = einsum_hi('fka,afl->fkl', bim, ebre) - einsum_hi('fka,afl->fkl', bre, ebim)
    return (residual_real, residual_imaginary, kernel_phase_real, kernel_phase_imaginary)

def reference(strips, sub_offset, uv_cells, measured):
    facet_count = N_FACET
    flattened_offsets = sub_offset.reshape(SUBGRID_TOTAL)
    flattened_uv_cells = uv_cells.reshape(SUBGRID_TOTAL, 2, VIS_PER_SUBGRID)
    flattened_measured = measured.reshape(SUBGRID_TOTAL, 2, VIS_PER_SUBGRID)

    def single_subgrid(input_arrays):
        subgrid_index, grid_offset, uv_points, measured_vis = input_arrays
        column = (subgrid_index // SG_COL).astype(jnp.int32)
        block_slice = lax.dynamic_slice_in_dim(strips, (column * CONTRIB_WIDTH).astype(jnp.int32), CONTRIB_WIDTH, 2)
        vis_real, vis_imaginary = facet_strip_kernel(grid_offset, CONTRIB_WIDTH, FACET_STRIP_LEN)
        kernel_real, kernel_imaginary = complex_product(block_slice[:, 0].reshape(facet_count * CONTRIB_WIDTH, FACET_STRIP_LEN), block_slice[:, 1].reshape(facet_count * CONTRIB_WIDTH, FACET_STRIP_LEN), vis_real, vis_imaginary)
        residual_real, residual_imaginary, kernel_phase_real, kernel_phase_imaginary = subgrid_update(kernel_real.reshape(facet_count, CONTRIB_WIDTH, CONTRIB_WIDTH), kernel_imaginary.reshape(facet_count, CONTRIB_WIDTH, CONTRIB_WIDTH), uv_points[0], uv_points[1], measured_vis[0], measured_vis[1], facet_count)
        return (jnp.stack([residual_real, residual_imaginary]), jnp.stack([kernel_phase_real, kernel_phase_imaginary], axis=1))
    residual_output, back_projection = lax.map(single_subgrid, (jnp.arange(SUBGRID_TOTAL, dtype=jnp.int32), flattened_offsets, flattened_uv_cells, flattened_measured))
    residual_vis = residual_output.reshape(COLS, SG_COL, 2, VIS_PER_SUBGRID)
    back_projection = back_projection.reshape(COLS, SG_COL, facet_count, 2, CONTRIB_WIDTH, CONTRIB_WIDTH)
    high_precision = lax.Precision.HIGHEST

    def column_step(carry, input_arrays):
        col, offsets, returned = input_arrays

        def add_item(acc, item):
            grid_offset, piece = item
            vis_real, vis_imaginary = facet_strip_kernel(grid_offset, CONTRIB_WIDTH, FACET_STRIP_LEN)
            phase_real = piece[:, 0].reshape(facet_count * CONTRIB_WIDTH, CONTRIB_WIDTH)
            phase_imaginary = piece[:, 1].reshape(facet_count * CONTRIB_WIDTH, CONTRIB_WIDTH)
            right_real = jnp.dot(phase_real, vis_real.T, precision=high_precision, preferred_element_type=jnp.float32) + jnp.dot(phase_imaginary, vis_imaginary.T, precision=high_precision, preferred_element_type=jnp.float32)
            right_imaginary = jnp.dot(phase_imaginary, vis_real.T, precision=high_precision, preferred_element_type=jnp.float32) - jnp.dot(phase_real, vis_imaginary.T, precision=high_precision, preferred_element_type=jnp.float32)
            return ((acc[0] + right_real, acc[1] + right_imaginary), None)
        zero = jnp.zeros((facet_count * CONTRIB_WIDTH, FACET_STRIP_LEN), jnp.float32)
        (right_real, right_imaginary), _ = lax.scan(add_item, (zero, zero), (offsets, returned))
        right_real = right_real.reshape(facet_count, CONTRIB_WIDTH, FACET_STRIP_LEN)
        right_imaginary = right_imaginary.reshape(facet_count, CONTRIB_WIDTH, FACET_STRIP_LEN)
        rows = jnp.arange(FR, dtype=jnp.int32)[:, None]
        keys = jnp.arange(CONTRIB_WIDTH, dtype=jnp.int32)[None, :] + CONTRIB_WIDTH * col
        cosine, sine = phase_terms(rows * keys, FR)
        phase_real = cosine / math.sqrt(FR)
        phase_imaginary = sine / math.sqrt(FR)
        dre = einsum_hi('rk,fkw->frw', phase_real, right_real) - einsum_hi('rk,fkw->frw', phase_imaginary, right_imaginary)
        dim = einsum_hi('rk,fkw->frw', phase_real, right_imaginary) + einsum_hi('rk,fkw->frw', phase_imaginary, right_real)
        return ((carry[0] + dre, carry[1] + dim), None)
    start = jnp.zeros((facet_count, FR, FACET_STRIP_LEN), jnp.float32)
    (dre, dim), _ = lax.scan(column_step, (start, start), (jnp.arange(COLS, dtype=jnp.int32), sub_offset, back_projection))
    dirty_image = jnp.stack([dre, dim], axis=1)
    return (dirty_image, residual_vis)
```

```python
import math

import jax
import jax.numpy as jnp
import numpy as np
from jax import lax
from jax.sharding import PartitionSpec as P

SUBGRID_SIZE = 256
HIGH = lax.Precision.HIGH


def unit(numer, denom):
    angle = (np.asarray(numer) % denom) * (2.0 * math.pi / denom)
    return np.exp(1j * angle)


def pick_table(facets, width):
    total = facets * width
    cells = np.arange(SUBGRID_SIZE)
    factor = (facets * width * width) ** -0.25
    e = factor * unit(np.arange(total)[:, None] * cells[None, :], total)
    h = e @ unit(-cells[:, None] * cells[None, :], SUBGRID_SIZE)
    h = h.reshape(facets, width, SUBGRID_SIZE)
    return np.concatenate([h.real, h.imag], axis=1).astype(np.float32)


def dot(a, b):
    return jnp.dot(a, b, precision=HIGH, preferred_element_type=jnp.float32)


def body(strips, sub_offset, uv_cells, measured):
    facets = lax.axis_size("facet")
    ncol = lax.axis_size("col")
    f = lax.axis_index("facet")
    c = lax.axis_index("col")
    width, length = strips.shape[2], strips.shape[3]
    per_col = sub_offset.shape[1]
    vis = uv_cells.shape[3]
    rows_all = width * ncol
    xr, xi = strips[0, 0], strips[0, 1]

    uv = lax.all_gather(uv_cells, "facet", axis=1, tiled=True)
    uv = lax.all_gather(uv, "col", axis=0, tiled=True)
    h = lax.dynamic_index_in_dim(jnp.asarray(pick_table(facets, width)), f, 0, keepdims=False)
    cells = jnp.arange(SUBGRID_SIZE, dtype=jnp.int32)[:, None]
    pick_u = (cells == uv[:, :, 0].reshape(1, -1)).astype(jnp.float32)
    pick_v = (cells == uv[:, :, 1].reshape(1, -1)).astype(jnp.float32)
    gv = dot(h, pick_v).reshape(2, width, ncol, per_col, vis)
    own_u = lax.dynamic_slice_in_dim(pick_u, c * per_col * vis, per_col * vis, 1)
    gu = dot(h, own_u).reshape(2, width, per_col, vis)
    own_v = lax.dynamic_index_in_dim(gv, c, 2, keepdims=False)

    j = jnp.arange(length, dtype=jnp.int32)
    ang = ((sub_offset.reshape(-1, 1) * j[None, :]) % length).astype(jnp.float32) * (2.0 * math.pi / length)
    pr, pi = jnp.cos(ang), jnp.sin(ang)
    w = unit(np.arange(length)[:, None] * np.arange(width)[None, :], length) / math.sqrt(length)
    wr, wi = np.real(w).astype(np.float32), np.imag(w).astype(np.float32)
    opr = lax.dynamic_slice_in_dim(pr, c * per_col, per_col, 0)[:, None, :]
    opi = lax.dynamic_slice_in_dim(pi, c * per_col, per_col, 0)[:, None, :]
    sr = (xr[None] * opr + xi[None] * opi).reshape(per_col * width, length)
    si = (xi[None] * opr - xr[None] * opi).reshape(per_col * width, length)
    wide = np.concatenate([wr, -wi], axis=1), np.concatenate([wi, wr], axis=1)
    k = dot(sr, wide[0]) + dot(si, wide[1])
    kr = k[:, :width].reshape(per_col, width, width)
    ki = k[:, width:].reshape(per_col, width, width)

    def bdot(a, b):
        return jnp.einsum("skl,lsv->skv", a, b, precision=HIGH, preferred_element_type=jnp.float32)

    ar = bdot(kr, own_v[0]) - bdot(ki, own_v[1])
    ai = bdot(kr, own_v[1]) + bdot(ki, own_v[0])
    gur, gui = gu[0].transpose(1, 0, 2), gu[1].transpose(1, 0, 2)
    part_r = jnp.sum(ar * gur - ai * gui, axis=1) / SUBGRID_SIZE
    part_i = jnp.sum(ar * gui + ai * gur, axis=1) / SUBGRID_SIZE
    part = -jnp.stack([part_r, part_i], axis=1)
    per_dev = measured.shape[1]
    mine = lax.dynamic_slice_in_dim(part, f * per_dev, per_dev, 0) + measured[0]
    part = lax.dynamic_update_slice_in_dim(part, mine, f * per_dev, 0)
    every = jnp.zeros((ncol,) + part.shape, jnp.float32)
    every = lax.dynamic_update_slice_in_dim(every, part[None], c, 0)
    res = lax.psum(every, ("facet", "col"))
    residual_vis = lax.dynamic_slice(res, (c, f * per_dev, 0, 0), (1, per_dev, 2, vis))

    r = np.arange(rows_all)
    p = unit(r[:, None] * r[None, :], rows_all) / math.sqrt(rows_all)
    p = p.reshape(ncol, width, ncol, width).transpose(0, 2, 1, 3)
    pmr = np.concatenate([p.real, p.imag], axis=3)
    pmi = np.concatenate([p.imag, -p.real], axis=3)
    pm = np.concatenate([pmr, pmi], axis=2).astype(np.float32)
    pm = lax.dynamic_index_in_dim(jnp.asarray(pm), c, 0, keepdims=False)
    ph = dot(pm.reshape(ncol * 2 * width, 2 * width), h).reshape(ncol, 2 * width, SUBGRID_SIZE)
    pg = jnp.einsum(
        "cru,ucx->crx", ph, pick_u.reshape(SUBGRID_SIZE, ncol, per_col * vis),
        precision=HIGH, preferred_element_type=jnp.float32,
    ).reshape(ncol, 2, width, per_col, vis)
    rr, ri = res[:, None, :, 0], res[:, None, :, 1]
    qr = pg[:, 0] * rr - pg[:, 1] * ri
    qi = pg[:, 0] * ri + pg[:, 1] * rr
    q = jnp.concatenate([qr, qi], axis=1)

    def adot(a, b):
        return jnp.einsum("crsv,lcsv->cslr", a, b, precision=HIGH, preferred_element_type=jnp.float32)

    dgr, dgi = adot(q, gv[0]), adot(q, gv[1])
    dr = dgr[..., :width] + dgi[..., width:]
    di = dgr[..., width:] - dgi[..., :width]
    left = jnp.concatenate([dr, di], -1).reshape(ncol, -1, 2 * width)
    right = jnp.concatenate([-di, dr], -1).reshape(ncol, -1, 2 * width)

    def add_column(acc, item):
        l, r, cr, ci = item
        vr = (cr[:, None, :] * wr.T[None] - ci[:, None, :] * wi.T[None]).reshape(-1, length)
        vi = (cr[:, None, :] * wi.T[None] + ci[:, None, :] * wr.T[None]).reshape(-1, length)
        return acc + dot(l.T, vr) + dot(r.T, vi), None

    shape = (ncol, per_col, length)
    image, _ = lax.scan(
        add_column,
        jnp.zeros((2 * width, length), jnp.float32),
        (left, right, pr.reshape(shape), pi.reshape(shape)),
    )
    return image.reshape(1, 2, width, length), residual_vis


def solution(mesh):
    return jax.shard_map(
        body,
        mesh=mesh,
        in_specs=(
            P("facet", None, "col", None),
            P(),
            P("col", "facet", None, None),
            P("col", "facet", None, None),
        ),
        out_specs=(P("facet", None, "col", None), P("col", "facet", None, None)),
        check_vma=False,
    )
```

```python
import math

import jax
import jax.numpy as jnp
import numpy as np
from jax import lax
from jax.experimental import pallas as pl
from jax.experimental.pallas import tpu as pltpu
from jax.sharding import PartitionSpec as P

SUBGRID_SIZE = 256
HIGH = lax.Precision.HIGH


def unit(numer, denom):
    angle = (np.asarray(numer) % denom) * (2.0 * math.pi / denom)
    return np.exp(1j * angle)


def pick_table(facets, width):
    total = facets * width
    cells = np.arange(SUBGRID_SIZE)
    factor = (facets * width * width) ** -0.25
    e = factor * unit(np.arange(total)[:, None] * cells[None, :], total)
    h = e @ unit(-cells[:, None] * cells[None, :], SUBGRID_SIZE)
    h = h.reshape(facets, width, SUBGRID_SIZE)
    return np.concatenate([h.real, h.imag], axis=1).astype(np.float32)


def dot(a, b):
    return jnp.dot(a, b, precision=HIGH, preferred_element_type=jnp.float32)


def split(x):
    hi = x.astype(jnp.bfloat16)
    return hi, (x - hi.astype(jnp.float32)).astype(jnp.bfloat16)


def dot3(a, b, dims):
    def one(x, y):
        return lax.dot_general(x, y, (dims, ((), ())), preferred_element_type=jnp.float32)

    (ah, al), (bh, bl) = split(a), split(b)
    return one(ah, bh) + (one(ah, bl) + one(al, bh))


def exchange_kernel(facets, ncol, add, x_ref, o_ref, slots, held, s1, r1, s2, r2):
    f = lax.axis_index("facet")
    c = lax.axis_index("col")
    mesh_id = pl.DeviceIdType.MESH
    barrier = pltpu.get_barrier_semaphore()
    for d in range(1, facets):
        pl.semaphore_signal(barrier, inc=1, device_id=(lax.rem(f + d, facets), c), device_id_type=mesh_id)
    for d in range(1, ncol):
        pl.semaphore_signal(barrier, inc=1, device_id=(f, lax.rem(c + d, ncol)), device_id_type=mesh_id)
    pl.semaphore_wait(barrier, facets + ncol - 2)
    copies = []
    for d in range(1, facets):
        copies.append(
            pltpu.make_async_remote_copy(
                src_ref=x_ref,
                dst_ref=slots.at[d - 1],
                send_sem=s1.at[d - 1],
                recv_sem=r1.at[d - 1],
                device_id=(lax.rem(f + d, facets), c),
                device_id_type=mesh_id,
            )
        )
        copies[-1].start()
    total = x_ref[...]
    if not add:
        held[c, f] = total
    for d in range(1, facets):
        copies[d - 1].wait_recv()
        if add:
            total = total + slots[d - 1]
        else:
            held[c, lax.rem(f - d + facets, facets)] = slots[d - 1]
    if add:
        held[c] = total
    later = []
    for d in range(1, ncol):
        later.append(
            pltpu.make_async_remote_copy(
                src_ref=held.at[c],
                dst_ref=held.at[c],
                send_sem=s2.at[d - 1],
                recv_sem=r2.at[d - 1],
                device_id=(f, lax.rem(c + d, ncol)),
                device_id_type=mesh_id,
            )
        )
        later[-1].start()
    for copy in copies:
        copy.wait_send()
    for copy in later:
        copy.wait()
    o_ref[...] = held[...]


def exchange(x, facets, ncol, add, collective_id):
    shape = (ncol,) + (x.shape if add else (facets,) + x.shape)
    return pl.pallas_call(
        lambda *refs: exchange_kernel(facets, ncol, add, *refs),
        out_shape=jax.ShapeDtypeStruct(shape, x.dtype),
        in_specs=[pl.BlockSpec(memory_space=pltpu.VMEM)],
        out_specs=pl.BlockSpec(memory_space=pltpu.VMEM),
        scratch_shapes=[
            pltpu.VMEM((facets - 1,) + x.shape, x.dtype),
            pltpu.VMEM(shape, x.dtype),
            pltpu.SemaphoreType.DMA((facets - 1,)),
            pltpu.SemaphoreType.DMA((facets - 1,)),
            pltpu.SemaphoreType.DMA((ncol - 1,)),
            pltpu.SemaphoreType.DMA((ncol - 1,)),
        ],
        compiler_params=pltpu.CompilerParams(collective_id=collective_id, has_side_effects=True),
    )(x)


def small_dft(terms):
    n = len(terms)
    if n == 1:
        return terms
    even, odd = small_dft(terms[::2]), small_dft(terms[1::2])
    first, second = [], []
    for j in range(n // 2):
        (er, ei), (r, i) = even[j], odd[j]
        if 4 * j == n:
            r, i = -i, r
        elif j:
            a, b = math.cos(2 * math.pi * j / n), math.sin(2 * math.pi * j / n)
            r, i = r * a - i * b, r * b + i * a
        first.append((er + r, ei + i))
        second.append((er - r, ei - i))
    return first + second


def image_kernel(res_ref, pg_ref, gv_ref, place_ref, wave_ref, turn_ref, o_ref, d_ref, grid_ref):
    ncol, per_col, _, vis = res_ref.shape
    width = gv_ref.shape[1] // 2
    length = o_ref.shape[1]
    lanes = wave_ref.shape[0]
    grid_ref[...] = jnp.zeros_like(grid_ref)

    def column(c, carry):
        for s in range(per_col):
            span = slice(s * vis, (s + 1) * vis)
            rr, ri = res_ref[c, s, 0:1, :], res_ref[c, s, 1:2, :]
            pr, pi = pg_ref[c, :width, span], pg_ref[c, width:, span]
            qr, qi = pr * rr - pi * ri, pr * ri + pi * rr
            q = jnp.concatenate(
                [jnp.concatenate([qr, qi], axis=1), jnp.concatenate([qi, -qr], axis=1)], axis=0
            )
            g = jnp.concatenate([gv_ref[c, :width, span], gv_ref[c, width:, span]], axis=1)
            d_ref[s * width : (s + 1) * width, :] = dot3(g, q, ((1,), (1,)))
        spots = lax.broadcasted_iota(jnp.int32, (per_col * width, length), 1)
        hot = jnp.where(spots == place_ref[c], 1.0, 0.0).astype(jnp.bfloat16)
        dims = (((1,), (0,)), ((), ()))
        for part in split(d_ref[...].T):
            grid_ref[...] += lax.dot_general(part, hot, dims, preferred_element_type=jnp.float32)
        return carry

    lax.fori_loop(0, ncol, column, 0)
    terms = []
    for rho in range(length // lanes):
        z = dot3(grid_ref[:, rho * lanes : (rho + 1) * lanes], wave_ref[...], ((1,), (0,)))
        zr = z[:width, :lanes] - z[width:, lanes:]
        zi = z[:width, lanes:] + z[width:, :lanes]
        tr, ti = turn_ref[rho : rho + 1, :lanes], turn_ref[rho : rho + 1, lanes:]
        terms.append((zr * tr - zi * ti, zr * ti + zi * tr))
    for j, (r, i) in enumerate(small_dft(terms)):
        o_ref[:width, j * lanes : (j + 1) * lanes] = r
        o_ref[width:, j * lanes : (j + 1) * lanes] = i


def form_image(res, pg, gv, offsets, width, length):
    lanes = 128
    blocks = length // lanes
    ncol, per_col = offsets.shape
    n = (offsets[:, :, None] + jnp.arange(width, dtype=jnp.int32)) % length
    place = ((n % blocks) * lanes + n // blocks).reshape(ncol, per_col * width, 1)
    k = np.arange(lanes)
    wave = unit(k[:, None] * k[None, :], lanes) / math.sqrt(length)
    turn = unit(np.arange(blocks)[:, None] * k[None, :], length)
    return pl.pallas_call(
        image_kernel,
        out_shape=jax.ShapeDtypeStruct((2 * width, length), jnp.float32),
        in_specs=[pl.BlockSpec(memory_space=pltpu.VMEM)] * 6,
        out_specs=pl.BlockSpec(memory_space=pltpu.VMEM),
        scratch_shapes=[
            pltpu.VMEM((per_col * width, 2 * width), jnp.float32),
            pltpu.VMEM((2 * width, length), jnp.float32),
        ],
        compiler_params=pltpu.CompilerParams(vmem_limit_bytes=48 * 2**20),
    )(
        res,
        pg,
        gv,
        place,
        jnp.asarray(np.concatenate([wave.real, wave.imag], axis=1).astype(np.float32)),
        jnp.asarray(np.concatenate([turn.real, turn.imag], axis=1).astype(np.float32)),
    )


def body(strips, sub_offset, uv_cells, measured):
    facets = lax.axis_size("facet")
    ncol = lax.axis_size("col")
    f = lax.axis_index("facet")
    c = lax.axis_index("col")
    width, length = strips.shape[2], strips.shape[3]
    per_col = sub_offset.shape[1]
    vis = uv_cells.shape[3]
    rows_all = width * ncol
    xr, xi = strips[0, 0], strips[0, 1]

    uv = exchange(uv_cells[0], facets, ncol, False, 1).reshape(ncol, per_col, 2, vis)
    h = lax.dynamic_index_in_dim(jnp.asarray(pick_table(facets, width)), f, 0, keepdims=False)
    cells = jnp.arange(SUBGRID_SIZE, dtype=jnp.int32)[:, None]
    pick_u = (cells == uv[:, :, 0].reshape(1, -1)).astype(jnp.float32)
    pick_v = (cells == uv[:, :, 1].reshape(1, -1)).astype(jnp.float32)
    gv = jnp.einsum(
        "ku,ucx->ckx", h, pick_v.reshape(SUBGRID_SIZE, ncol, per_col * vis),
        precision=HIGH, preferred_element_type=jnp.float32,
    )
    own_u = lax.dynamic_slice_in_dim(pick_u, c * per_col * vis, per_col * vis, 1)
    gu = dot(h, own_u).reshape(2, width, per_col, vis)
    own_v = lax.dynamic_index_in_dim(gv, c, 0, keepdims=False).reshape(2, width, per_col, vis)

    j = jnp.arange(length, dtype=jnp.int32)
    own = lax.dynamic_index_in_dim(sub_offset, c, 0, keepdims=False)
    ang = ((own[:, None] * j[None, :]) % length).astype(jnp.float32) * (2.0 * math.pi / length)
    pr, pi = jnp.cos(ang), jnp.sin(ang)
    w = unit(np.arange(length)[:, None] * np.arange(width)[None, :], length) / math.sqrt(length)
    wr, wi = np.real(w).astype(np.float32), np.imag(w).astype(np.float32)
    opr, opi = pr[:, None, :], pi[:, None, :]
    sr = (xr[None] * opr + xi[None] * opi).reshape(per_col * width, length)
    si = (xi[None] * opr - xr[None] * opi).reshape(per_col * width, length)
    wide = np.concatenate([wr, -wi], axis=1), np.concatenate([wi, wr], axis=1)
    k = dot(sr, wide[0]) + dot(si, wide[1])
    kr = k[:, :width].reshape(per_col, width, width)
    ki = k[:, width:].reshape(per_col, width, width)

    def bdot(a, b):
        return jnp.einsum("skl,lsv->skv", a, b, precision=HIGH, preferred_element_type=jnp.float32)

    ar = bdot(kr, own_v[0]) - bdot(ki, own_v[1])
    ai = bdot(kr, own_v[1]) + bdot(ki, own_v[0])
    gur, gui = gu[0].transpose(1, 0, 2), gu[1].transpose(1, 0, 2)
    part_r = jnp.sum(ar * gur - ai * gui, axis=1) / SUBGRID_SIZE
    part_i = jnp.sum(ar * gui + ai * gur, axis=1) / SUBGRID_SIZE
    part = -jnp.stack([part_r, part_i], axis=1)
    per_dev = measured.shape[1]
    mine = lax.dynamic_slice_in_dim(part, f * per_dev, per_dev, 0) + measured[0]
    part = lax.dynamic_update_slice_in_dim(part, mine, f * per_dev, 0)
    res = exchange(part, facets, ncol, True, 2)
    residual_vis = lax.dynamic_slice(res, (c, f * per_dev, 0, 0), (1, per_dev, 2, vis))

    r = np.arange(rows_all)
    p = unit(r[:, None] * r[None, :], rows_all) / math.sqrt(rows_all)
    p = p.reshape(ncol, width, ncol, width).transpose(0, 2, 1, 3)
    pmr = np.concatenate([p.real, p.imag], axis=3)
    pmi = np.concatenate([p.imag, -p.real], axis=3)
    pm = np.concatenate([pmr, pmi], axis=2).astype(np.float32)
    pm = lax.dynamic_index_in_dim(jnp.asarray(pm), c, 0, keepdims=False)
    ph = dot(pm.reshape(ncol * 2 * width, 2 * width), h).reshape(ncol, 2 * width, SUBGRID_SIZE)
    pg = jnp.einsum(
        "cru,ucx->crx", ph, pick_u.reshape(SUBGRID_SIZE, ncol, per_col * vis),
        precision=HIGH, preferred_element_type=jnp.float32,
    )
    image = form_image(res, pg, gv, sub_offset, width, length)
    return image.reshape(1, 2, width, length), residual_vis


def solution(mesh):
    return jax.shard_map(
        body,
        mesh=mesh,
        in_specs=(
            P("facet", None, "col", None),
            P(),
            P("col", "facet", None, None),
            P("col", "facet", None, None),
        ),
        out_specs=(P("facet", None, "col", None), P("col", "facet", None, None)),
        check_vma=False,
    )
```

```python
import math

import jax
import jax.numpy as jnp
import numpy as np
from jax import lax
from jax.experimental import pallas as pl
from jax.experimental.pallas import tpu as pltpu
from jax.sharding import PartitionSpec as P

SUBGRID_SIZE = 256
HIGH = lax.Precision.HIGH


def unit(numer, denom):
    angle = (np.asarray(numer) % denom) * (2.0 * math.pi / denom)
    return np.exp(1j * angle)


def pick_table(facets, width):
    total = facets * width
    cells = np.arange(SUBGRID_SIZE)
    factor = (facets * width * width) ** -0.25
    e = factor * unit(np.arange(total)[:, None] * cells[None, :], total)
    h = e @ unit(-cells[:, None] * cells[None, :], SUBGRID_SIZE)
    h = h.reshape(facets, width, SUBGRID_SIZE)
    return np.concatenate([h.real, h.imag], axis=1).astype(np.float32)


def dot(a, b):
    return jnp.dot(a, b, precision=HIGH, preferred_element_type=jnp.float32)


def split(x):
    hi = x.astype(jnp.bfloat16)
    return hi, (x - hi.astype(jnp.float32)).astype(jnp.bfloat16)


def dot3(a, b, dims):
    def one(x, y):
        return lax.dot_general(x, y, (dims, ((), ())), preferred_element_type=jnp.float32)

    (ah, al), (bh, bl) = split(a), split(b)
    return one(ah, bh) + (one(ah, bl) + one(al, bh))


def placed(offsets, width, length, lanes):
    blocks = length // lanes
    steps = lax.broadcasted_iota(jnp.int32, (width, 1), 0)
    cells = [(offsets[s : s + 1, :] + steps) & (length - 1) for s in range(offsets.shape[0])]
    n = jnp.concatenate(cells, axis=0)
    spot = (n & (blocks - 1)) * lanes + (n >> (blocks.bit_length() - 1))
    spots = lax.broadcasted_iota(jnp.int32, (n.shape[0], length), 1)
    return jnp.where(spots == spot, 1.0, 0.0).astype(jnp.bfloat16)


def picked(parts, index):
    cells = lax.broadcasted_iota(jnp.int32, (SUBGRID_SIZE, index.shape[1]), 0)
    hot = jnp.where(cells == index, 1.0, 0.0).astype(jnp.bfloat16)
    dims = (((1,), (0,)), ((), ()))
    high, low = [lax.dot_general(p, hot, dims, preferred_element_type=jnp.float32) for p in parts]
    return high + low


def predict_kernel(
    facets, ncol, x_ref, uv_ref, meas_ref, off_ref, h_ref, wave_ref, turn_ref,
    res_ref, all_uv_ref, own_ref,
    uv_slots, uv_held, part_ref, slots, held, grid_ref, kt_ref, s1, r1, s2, r2, s3, r3, s4, r4,
):
    f = lax.axis_index("facet")
    c = lax.axis_index("col")
    mesh_id = pl.DeviceIdType.MESH
    width, length = x_ref.shape[1], x_ref.shape[2]
    lanes = wave_ref.shape[0]
    blocks = length // lanes

    def over_facets(src, dst, send, recv):
        copies = [
            pltpu.make_async_remote_copy(
                src_ref=src,
                dst_ref=dst.at[d - 1],
                send_sem=send.at[d - 1],
                recv_sem=recv.at[d - 1],
                device_id=(lax.rem(f + d, facets), c),
                device_id_type=mesh_id,
            )
            for d in range(1, facets)
        ]
        for copy in copies:
            copy.start()
        return copies

    def over_columns(ref, send, recv):
        copies = [
            pltpu.make_async_remote_copy(
                src_ref=ref.at[c],
                dst_ref=ref.at[c],
                send_sem=send.at[d - 1],
                recv_sem=recv.at[d - 1],
                device_id=(f, lax.rem(c + d, ncol)),
                device_id_type=mesh_id,
            )
            for d in range(1, ncol)
        ]
        for copy in copies:
            copy.start()
        return copies

    barrier = pltpu.get_barrier_semaphore()
    for d in range(1, facets):
        pl.semaphore_signal(barrier, inc=1, device_id=(lax.rem(f + d, facets), c), device_id_type=mesh_id)
    for d in range(1, ncol):
        pl.semaphore_signal(barrier, inc=1, device_id=(f, lax.rem(c + d, ncol)), device_id_type=mesh_id)
    pl.semaphore_wait(barrier, facets + ncol - 2)
    uv_copies = over_facets(uv_ref, uv_slots, s1, r1)

    spans = [slice(i * lanes, (i + 1) * lanes) for i in range(blocks)]
    for rho, (yr, yi) in enumerate(small_dft([(x_ref[0, :, i], -x_ref[1, :, i]) for i in spans])):
        tr, ti = turn_ref[rho : rho + 1, :lanes], turn_ref[rho : rho + 1, lanes:]
        z = jnp.concatenate([yr * tr - yi * ti, yr * ti + yi * tr], axis=0)
        p = dot3(z, wave_ref[...], ((1,), (0,)))
        grid_ref[:width, spans[rho]] = p[:width, :lanes] - p[width:, lanes:]
        grid_ref[width:, spans[rho]] = -(p[:width, lanes:] + p[width:, :lanes])
    hot = placed(off_ref[c], width, length, lanes)
    dims = (((1,), (1,)), ((), ()))
    high, low = [
        lax.dot_general(hot, part, dims, preferred_element_type=jnp.float32)
        for part in split(grid_ref[...])
    ]
    kt_ref[...] = high + low

    uv_held[c, f] = uv_ref[...]
    for d in range(1, facets):
        uv_copies[d - 1].wait_recv()
        uv_held[c, lax.rem(f - d + facets, facets)] = uv_slots[d - 1]
    uv_later = over_columns(uv_held, s2, r2)

    parts = split(h_ref[f])
    for s in range(facets):
        gu = picked(parts, uv_held[c, s, 0:1, :])
        gv = picked(parts, uv_held[c, s, 1:2, :])
        gur, gui, gvr, gvi = gu[:width], gu[width:], gv[:width], gv[width:]
        wide = jnp.concatenate(
            [jnp.concatenate([gur, gui], axis=1), jnp.concatenate([-gui, gur], axis=1)], axis=0
        )
        a = dot3(kt_ref[s * width : (s + 1) * width, :], wide, ((1,), (0,)))
        vis = gu.shape[1]
        ar, ai = a[:, :vis], a[:, vis:]
        pr = jnp.sum(ar * gvr - ai * gvi, axis=0, keepdims=True)
        pi = jnp.sum(ar * gvi + ai * gvr, axis=0, keepdims=True)
        pred = jnp.concatenate([pr, pi], axis=0) * (1.0 / SUBGRID_SIZE)
        part_ref[s] = jnp.where(f == s, meas_ref[...], 0.0) - pred

    copies = over_facets(part_ref, slots, s3, r3)
    total = part_ref[...]
    for d in range(1, facets):
        copies[d - 1].wait_recv()
        total = total + slots[d - 1]
    held[c] = total
    later = over_columns(held, s4, r4)
    own_ref[...] = held[c, f]
    for copy in uv_copies + copies:
        copy.wait_send()
    for copy in uv_later:
        copy.wait()
    all_uv_ref[...] = uv_held[...]
    for copy in later:
        copy.wait()
    res_ref[...] = held[...]


def predict(x, uv, measured, offsets, h, wave, turn, facets, ncol):
    width, length = x.shape[1:]
    pair = uv.shape
    full = (ncol, facets) + pair
    dma = pltpu.SemaphoreType.DMA
    return pl.pallas_call(
        lambda *refs: predict_kernel(facets, ncol, *refs),
        out_shape=(
            jax.ShapeDtypeStruct(full, jnp.float32),
            jax.ShapeDtypeStruct(full, jnp.int32),
            jax.ShapeDtypeStruct(pair, jnp.float32),
        ),
        in_specs=[pl.BlockSpec(memory_space=pltpu.VMEM)] * 7,
        out_specs=[pl.BlockSpec(memory_space=pltpu.VMEM)] * 3,
        scratch_shapes=[
            pltpu.VMEM((facets - 1,) + pair, jnp.int32),
            pltpu.VMEM(full, jnp.int32),
            pltpu.VMEM((facets,) + pair, jnp.float32),
            pltpu.VMEM((facets - 1, facets) + pair, jnp.float32),
            pltpu.VMEM(full, jnp.float32),
            pltpu.VMEM((2 * width, length), jnp.float32),
            pltpu.VMEM((facets * width, 2 * width), jnp.float32),
        ]
        + [dma((facets - 1,))] * 2
        + [dma((ncol - 1,))] * 2
        + [dma((facets - 1,))] * 2
        + [dma((ncol - 1,))] * 2,
        compiler_params=pltpu.CompilerParams(
            collective_id=1, has_side_effects=True, vmem_limit_bytes=48 * 2**20
        ),
    )(x, uv, measured, offsets, h, wave, turn)


def small_dft(terms):
    n = len(terms)
    if n == 1:
        return terms
    even, odd = small_dft(terms[::2]), small_dft(terms[1::2])
    first, second = [], []
    for j in range(n // 2):
        (er, ei), (r, i) = even[j], odd[j]
        if 4 * j == n:
            r, i = -i, r
        elif j:
            a, b = math.cos(2 * math.pi * j / n), math.sin(2 * math.pi * j / n)
            r, i = r * a - i * b, r * b + i * a
        first.append((er + r, ei + i))
        second.append((er - r, ei - i))
    return first + second


def image_kernel(res_ref, uv_ref, off_ref, h_ref, pm_ref, wave_ref, turn_ref, o_ref, d_ref, grid_ref):
    ncol, per_col = res_ref.shape[:2]
    width = h_ref.shape[1] // 2
    h = h_ref[lax.axis_index("facet")]
    rows = lax.axis_index("col")
    parts = split(h)
    length = o_ref.shape[1]
    lanes = wave_ref.shape[0]
    grid_ref[...] = jnp.zeros_like(grid_ref)

    def column(c, carry):
        phase = split(dot3(pm_ref[rows, c], h, ((1,), (0,))))
        for s in range(per_col):
            pg = picked(phase, uv_ref[c, s, 0:1, :])
            gv = picked(parts, uv_ref[c, s, 1:2, :])
            rr, ri = res_ref[c, s, 0:1, :], res_ref[c, s, 1:2, :]
            pr, pi = pg[:width], pg[width:]
            qr, qi = pr * rr - pi * ri, pr * ri + pi * rr
            q = jnp.concatenate(
                [jnp.concatenate([qr, qi], axis=1), jnp.concatenate([qi, -qr], axis=1)], axis=0
            )
            g = jnp.concatenate([gv[:width], gv[width:]], axis=1)
            d_ref[s * width : (s + 1) * width, :] = dot3(g, q, ((1,), (1,)))
        hot = placed(off_ref[c], width, length, lanes)
        dims = (((1,), (0,)), ((), ()))
        for part in split(d_ref[...].T):
            grid_ref[...] += lax.dot_general(part, hot, dims, preferred_element_type=jnp.float32)
        return carry

    lax.fori_loop(0, ncol, column, 0)
    terms = []
    for rho in range(length // lanes):
        z = dot3(grid_ref[:, rho * lanes : (rho + 1) * lanes], wave_ref[...], ((1,), (0,)))
        zr = z[:width, :lanes] - z[width:, lanes:]
        zi = z[:width, lanes:] + z[width:, :lanes]
        tr, ti = turn_ref[rho : rho + 1, :lanes], turn_ref[rho : rho + 1, lanes:]
        terms.append((zr * tr - zi * ti, zr * ti + zi * tr))
    for j, (r, i) in enumerate(small_dft(terms)):
        o_ref[:width, j * lanes : (j + 1) * lanes] = r
        o_ref[width:, j * lanes : (j + 1) * lanes] = i


def form_image(res, uv, offsets, h, pm, wave, turn, width, length):
    per_col = offsets.shape[1]
    return pl.pallas_call(
        image_kernel,
        out_shape=jax.ShapeDtypeStruct((2 * width, length), jnp.float32),
        in_specs=[pl.BlockSpec(memory_space=pltpu.VMEM)] * 7,
        out_specs=pl.BlockSpec(memory_space=pltpu.VMEM),
        scratch_shapes=[
            pltpu.VMEM((per_col * width, 2 * width), jnp.float32),
            pltpu.VMEM((2 * width, length), jnp.float32),
        ],
        compiler_params=pltpu.CompilerParams(vmem_limit_bytes=48 * 2**20),
    )(res, uv, offsets, h, pm, wave, turn)


def sides(z, axis):
    return jnp.asarray(np.concatenate([z.real, z.imag], axis=axis).astype(np.float32))


def body(strips, sub_offset, uv_cells, measured):
    facets = lax.axis_size("facet")
    ncol = lax.axis_size("col")
    width, length = strips.shape[2], strips.shape[3]
    assert uv_cells.shape[1] == 1 and sub_offset.shape[1] == facets
    rows_all = width * ncol
    lanes = 128
    k = np.arange(lanes)
    wave = sides(unit(k[:, None] * k[None, :], lanes) / math.sqrt(length), 1)
    turn = sides(unit(np.arange(length // lanes)[:, None] * k[None, :], length), 1)
    h = jnp.asarray(pick_table(facets, width))
    r = np.arange(rows_all)
    p = unit(r[:, None] * r[None, :], rows_all) / math.sqrt(rows_all)
    p = p.reshape(ncol, width, ncol, width).transpose(0, 2, 1, 3)
    pm = np.concatenate(
        [
            np.concatenate([p.real, p.imag], axis=3),
            np.concatenate([p.imag, -p.real], axis=3),
        ],
        axis=2,
    ).astype(np.float32)
    offsets = sub_offset[:, :, None]
    res, uv, own = predict(
        strips[0], uv_cells[0, 0], measured[0, 0], offsets, h, wave, turn, facets, ncol
    )
    image = form_image(res, uv, offsets, h, jnp.asarray(pm), wave, turn, width, length)
    return image.reshape(1, 2, width, length), own[None, None]


def solution(mesh):
    return jax.shard_map(
        body,
        mesh=mesh,
        in_specs=(
            P("facet", None, "col", None),
            P(),
            P("col", "facet", None, None),
            P("col", "facet", None, None),
        ),
        out_specs=(P("facet", None, "col", None), P("col", "facet", None, None)),
        check_vma=False,
    )
```

```python
import math

import jax
import jax.numpy as jnp
import numpy as np
from jax import lax
from jax.experimental import pallas as pl
from jax.experimental.pallas import tpu as pltpu
from jax.sharding import PartitionSpec as P

SUBGRID_SIZE = 256
HIGH = lax.Precision.HIGH


def unit(numer, denom):
    angle = (np.asarray(numer) % denom) * (2.0 * math.pi / denom)
    return np.exp(1j * angle)


def pick_table(facets, width):
    total = facets * width
    cells = np.arange(SUBGRID_SIZE)
    factor = (facets * width * width) ** -0.25
    e = factor * unit(np.arange(total)[:, None] * cells[None, :], total)
    h = e @ unit(-cells[:, None] * cells[None, :], SUBGRID_SIZE)
    h = h.reshape(facets, width, SUBGRID_SIZE)
    return np.concatenate([h.real, h.imag], axis=1).astype(np.float32)


def dot(a, b):
    return jnp.dot(a, b, precision=HIGH, preferred_element_type=jnp.float32)


def split(x):
    hi = x.astype(jnp.bfloat16)
    return hi, (x - hi.astype(jnp.float32)).astype(jnp.bfloat16)


def dot3(a, b, dims):
    def one(x, y):
        return lax.dot_general(x, y, (dims, ((), ())), preferred_element_type=jnp.float32)

    (ah, al), (bh, bl) = split(a), split(b)
    return one(ah, bh) + (one(ah, bl) + one(al, bh))


def placed(offsets, width, length, lanes):
    blocks = length // lanes
    steps = lax.broadcasted_iota(jnp.int32, (width, 1), 0)
    cells = [(offsets[s : s + 1, :] + steps) & (length - 1) for s in range(offsets.shape[0])]
    n = jnp.concatenate(cells, axis=0)
    spot = (n & (blocks - 1)) * lanes + (n >> (blocks.bit_length() - 1))
    spots = lax.broadcasted_iota(jnp.int32, (n.shape[0], length), 1)
    return jnp.where(spots == spot, 1.0, 0.0).astype(jnp.bfloat16)


def picked(parts, index):
    cells = lax.broadcasted_iota(jnp.int32, (SUBGRID_SIZE, index.shape[1]), 0)
    hot = jnp.where(cells == index, 1.0, 0.0).astype(jnp.bfloat16)
    dims = (((1,), (0,)), ((), ()))
    both = lax.dot_general(parts, hot, dims, preferred_element_type=jnp.float32)
    return both[: both.shape[0] // 2] + both[both.shape[0] // 2 :]


def predict_kernel(
    facets, ncol, x_ref, uv_ref, meas_ref, off_ref, h_ref, pm_ref, wave_ref, turn_ref,
    o_ref, own_ref,
    uv_slots, uv_held, part_ref, slots, held, grid_ref, kt_ref, hot_ref, pg_ref, gv_ref, s1, r1, s2, r2, s3, r3, s4, r4,
):
    f = lax.axis_index("facet")
    c = lax.axis_index("col")
    mesh_id = pl.DeviceIdType.MESH
    width, length = x_ref.shape[1], x_ref.shape[2]
    lanes = wave_ref.shape[0]
    blocks = length // lanes

    def over_facets(src, dst, send, recv):
        copies = [
            pltpu.make_async_remote_copy(
                src_ref=src,
                dst_ref=dst.at[d - 1],
                send_sem=send.at[d - 1],
                recv_sem=recv.at[d - 1],
                device_id=(lax.rem(f + d, facets), c),
                device_id_type=mesh_id,
            )
            for d in range(1, facets)
        ]
        for copy in copies:
            copy.start()
        return copies

    def over_columns(ref, send, recv):
        copies = [
            pltpu.make_async_remote_copy(
                src_ref=ref.at[c],
                dst_ref=ref.at[c],
                send_sem=send.at[d - 1],
                recv_sem=recv.at[d - 1],
                device_id=(f, lax.rem(c + d, ncol)),
                device_id_type=mesh_id,
            )
            for d in range(1, ncol)
        ]
        for copy in copies:
            copy.start()
        return copies

    barrier = pltpu.get_barrier_semaphore()
    for d in range(1, facets):
        pl.semaphore_signal(barrier, inc=1, device_id=(lax.rem(f + d, facets), c), device_id_type=mesh_id)
    for d in range(1, ncol):
        pl.semaphore_signal(barrier, inc=1, device_id=(f, lax.rem(c + d, ncol)), device_id_type=mesh_id)
    pl.semaphore_wait(barrier, facets + ncol - 2)
    uv_copies = over_facets(uv_ref, uv_slots, s1, r1)

    spans = [slice(i * lanes, (i + 1) * lanes) for i in range(blocks)]
    for rho, (yr, yi) in enumerate(small_dft([(x_ref[0, :, i], -x_ref[1, :, i]) for i in spans])):
        tr, ti = turn_ref[rho : rho + 1, :lanes], turn_ref[rho : rho + 1, lanes:]
        z = jnp.concatenate([yr * tr - yi * ti, yr * ti + yi * tr], axis=0)
        p = dot3(z, wave_ref[...], ((1,), (0,)))
        grid_ref[:width, spans[rho]] = p[:width, :lanes] - p[width:, lanes:]
        grid_ref[width:, spans[rho]] = -(p[:width, lanes:] + p[width:, :lanes])
    hot_ref[c] = placed(off_ref[c], width, length, lanes)
    hot = hot_ref[c]
    dims = (((1,), (1,)), ((), ()))
    high, low = [
        lax.dot_general(hot, part, dims, preferred_element_type=jnp.float32)
        for part in split(grid_ref[...])
    ]
    kt_ref[...] = high + low

    uv_held[c, f] = uv_ref[...]
    for d in range(1, facets):
        uv_copies[d - 1].wait_recv()
        uv_held[c, lax.rem(f - d + facets, facets)] = uv_slots[d - 1]
    uv_later = over_columns(uv_held, s2, r2)

    parts = jnp.concatenate(split(h_ref[f]), axis=0)
    for s in range(facets):
        gu = picked(parts, uv_held[c, s, 0:1, :])
        gv = picked(parts, uv_held[c, s, 1:2, :])
        gur, gui, gvr, gvi = gu[:width], gu[width:], gv[:width], gv[width:]
        wide = jnp.concatenate(
            [jnp.concatenate([gur, gui], axis=1), jnp.concatenate([-gui, gur], axis=1)], axis=0
        )
        a = dot3(kt_ref[s * width : (s + 1) * width, :], wide, ((1,), (0,)))
        vis = gu.shape[1]
        ar, ai = a[:, :vis], a[:, vis:]
        pr = jnp.sum(ar * gvr - ai * gvi, axis=0, keepdims=True)
        pi = jnp.sum(ar * gvi + ai * gvr, axis=0, keepdims=True)
        pred = jnp.concatenate([pr, pi], axis=0) * (1.0 / SUBGRID_SIZE)
        part_ref[s] = jnp.where(f == s, meas_ref[...], 0.0) - pred

    copies = over_facets(part_ref, slots, s3, r3)

    def place_column(i, carry):
        col = lax.rem(c + i, ncol)
        hot_ref[col] = placed(off_ref[col], width, length, lanes)
        return carry

    lax.fori_loop(1, ncol, place_column, 0)
    total = part_ref[...]
    for d in range(1, facets):
        copies[d - 1].wait_recv()
        total = total + slots[d - 1]
    held[c] = total
    later = over_columns(held, s4, r4)
    own_ref[...] = held[c, f]
    for copy in uv_later:
        copy.wait()

    def pick_column(col, carry):
        phase = jnp.concatenate(split(dot3(pm_ref[c, col], h_ref[f], ((1,), (0,)))), axis=0)
        for s in range(facets):
            pg_ref[col, s] = picked(phase, uv_held[col, s, 0:1, :])
            gv_ref[col, s] = picked(parts, uv_held[col, s, 1:2, :])
        return carry

    lax.fori_loop(0, ncol, pick_column, 0)
    for copy in uv_copies + copies:
        copy.wait_send()
    for copy in later:
        copy.wait()
    grid_ref[...] = jnp.zeros_like(grid_ref)
    form_image(held, pg_ref, gv_ref, hot_ref, wave_ref, turn_ref, o_ref, kt_ref, grid_ref)


def predict(x, uv, measured, offsets, h, pm, wave, turn, facets, ncol):
    width, length = x.shape[1:]
    pair = uv.shape
    full = (ncol, facets) + pair
    dma = pltpu.SemaphoreType.DMA
    return pl.pallas_call(
        lambda *refs: predict_kernel(facets, ncol, *refs),
        out_shape=(
            jax.ShapeDtypeStruct((2 * width, length), jnp.float32),
            jax.ShapeDtypeStruct(pair, jnp.float32),
        ),
        in_specs=[pl.BlockSpec(memory_space=pltpu.VMEM)] * 8,
        out_specs=[pl.BlockSpec(memory_space=pltpu.VMEM)] * 2,
        scratch_shapes=[
            pltpu.VMEM((facets - 1,) + pair, jnp.int32),
            pltpu.VMEM(full, jnp.int32),
            pltpu.VMEM((facets,) + pair, jnp.float32),
            pltpu.VMEM((facets - 1, facets) + pair, jnp.float32),
            pltpu.VMEM(full, jnp.float32),
            pltpu.VMEM((2 * width, length), jnp.float32),
            pltpu.VMEM((facets * width, 2 * width), jnp.float32),
            pltpu.VMEM((ncol, facets * width, length), jnp.bfloat16),
            pltpu.VMEM((ncol, facets, 2 * width, pair[1]), jnp.float32),
            pltpu.VMEM((ncol, facets, 2 * width, pair[1]), jnp.float32),
        ]
        + [dma((facets - 1,))] * 2
        + [dma((ncol - 1,))] * 2
        + [dma((facets - 1,))] * 2
        + [dma((ncol - 1,))] * 2,
        compiler_params=pltpu.CompilerParams(
            collective_id=1, has_side_effects=True, vmem_limit_bytes=56 * 2**20
        ),
    )(x, uv, measured, offsets, h, pm, wave, turn)


def small_dft(terms):
    n = len(terms)
    if n == 1:
        return terms
    even, odd = small_dft(terms[::2]), small_dft(terms[1::2])
    first, second = [], []
    for j in range(n // 2):
        (er, ei), (r, i) = even[j], odd[j]
        if 4 * j == n:
            r, i = -i, r
        elif j:
            a, b = math.cos(2 * math.pi * j / n), math.sin(2 * math.pi * j / n)
            r, i = r * a - i * b, r * b + i * a
        first.append((er + r, ei + i))
        second.append((er - r, ei - i))
    return first + second


def form_image(res_ref, pg_ref, gv_ref, hot_ref, wave_ref, turn_ref, o_ref, d_ref, grid_ref):
    ncol, per_col = res_ref.shape[:2]
    width = o_ref.shape[0] // 2
    length = o_ref.shape[1]
    lanes = wave_ref.shape[0]

    def column(c, carry):
        for s in range(per_col):
            pg, gv = pg_ref[c, s], gv_ref[c, s]
            rr, ri = res_ref[c, s, 0:1, :], res_ref[c, s, 1:2, :]
            pr, pi = pg[:width], pg[width:]
            qr, qi = pr * rr - pi * ri, pr * ri + pi * rr
            q = jnp.concatenate(
                [jnp.concatenate([qr, qi], axis=1), jnp.concatenate([qi, -qr], axis=1)], axis=0
            )
            g = jnp.concatenate([gv[:width], gv[width:]], axis=1)
            d_ref[s * width : (s + 1) * width, :] = dot3(g, q, ((1,), (1,)))
        hot = hot_ref[c]
        dims = (((1,), (0,)), ((), ()))
        for part in split(d_ref[...].T):
            grid_ref[...] += lax.dot_general(part, hot, dims, preferred_element_type=jnp.float32)
        return carry

    lax.fori_loop(0, ncol, column, 0)
    terms = []
    for rho in range(length // lanes):
        z = dot3(grid_ref[:, rho * lanes : (rho + 1) * lanes], wave_ref[...], ((1,), (0,)))
        zr = z[:width, :lanes] - z[width:, lanes:]
        zi = z[:width, lanes:] + z[width:, :lanes]
        tr, ti = turn_ref[rho : rho + 1, :lanes], turn_ref[rho : rho + 1, lanes:]
        terms.append((zr * tr - zi * ti, zr * ti + zi * tr))
    for j, (r, i) in enumerate(small_dft(terms)):
        o_ref[:width, j * lanes : (j + 1) * lanes] = r
        o_ref[width:, j * lanes : (j + 1) * lanes] = i


def sides(z, axis):
    return jnp.asarray(np.concatenate([z.real, z.imag], axis=axis).astype(np.float32))


def body(strips, sub_offset, uv_cells, measured):
    facets = lax.axis_size("facet")
    ncol = lax.axis_size("col")
    width, length = strips.shape[2], strips.shape[3]
    assert uv_cells.shape[1] == 1 and sub_offset.shape[1] == facets
    rows_all = width * ncol
    lanes = 128
    k = np.arange(lanes)
    wave = sides(unit(k[:, None] * k[None, :], lanes) / math.sqrt(length), 1)
    turn = sides(unit(np.arange(length // lanes)[:, None] * k[None, :], length), 1)
    h = jnp.asarray(pick_table(facets, width))
    r = np.arange(rows_all)
    p = unit(r[:, None] * r[None, :], rows_all) / math.sqrt(rows_all)
    p = p.reshape(ncol, width, ncol, width).transpose(0, 2, 1, 3)
    pm = np.concatenate(
        [
            np.concatenate([p.real, p.imag], axis=3),
            np.concatenate([p.imag, -p.real], axis=3),
        ],
        axis=2,
    ).astype(np.float32)
    offsets = sub_offset[:, :, None]
    image, own = predict(
        strips[0], uv_cells[0, 0], measured[0, 0], offsets, h, jnp.asarray(pm), wave, turn, facets, ncol
    )
    return image.reshape(1, 2, width, length), own[None, None]


def solution(mesh):
    return jax.shard_map(
        body,
        mesh=mesh,
        in_specs=(
            P("facet", None, "col", None),
            P(),
            P("col", "facet", None, None),
            P("col", "facet", None, None),
        ),
        out_specs=(P("facet", None, "col", None), P("col", "facet", None, None)),
        check_vma=False,
    )
```
